32 devices in a mesh: groups: 2 (over y), dp: 1, expert: 16 (over z, x, core).
Axes of the slice: x: 2, y: 2, z: 4, core: 2. Of those that a mesh axis runs over, the one named last changes fastest.
Arguments:
- inner: bfloat16 [4096, 8, 384], P(('groups', 'dp', 'expert')), parts along dimension 0, may hold values from -0.59765625 to 0.59765625
- upstream: bfloat16 [4096, 2048], P(('groups', 'dp', 'expert')), parts along dimension 0, may hold values from -6 to 6
- routes: int32 [4096, 8], P(('groups', 'dp', 'expert')), parts along dimension 0, may hold values from 0 to 15, all different within a row; in each aligned block of 128 rows (0 to 127, 128 to 255, ...) at most 96 rows name the same one
- gates: float32 [4096, 8], P(('groups', 'dp', 'expert')), parts along dimension 0, may hold values from 0.2 to 1
- lengths: int32 [4], P('groups'), parts along dimension 0, may hold values from 1 to 1536, 2048 in all
- advantages: float32 [4], P('groups'), parts along dimension 0, may hold values from -4 to 4
- down_weight: bfloat16 [16, 2048, 384], P('expert', 'dp'), may hold values from -0.125 to 0.125
Outputs:
- grad_inner: bfloat16 [4096, 8, 384], P(('groups', 'dp', 'expert')), parts along dimension 0
- grad_down: bfloat16 [32, 2048, 384], P(('groups', 'expert'), 'dp'), parts along dimension 0
The draws below stay inside these ranges and needn't reach their ends.
There are 2 independent parts, one for each index of `groups`. The reference program is written for one: setup_inputs(seed, part) draws one part's arguments, and reference() takes and returns one part's arrays. A program takes and returns all parts, laid end to end along the dimension named above; an argument that names none is the same for every part. Nothing has to cross between parts.
Inputs may be any that keep to these rules, and one draw needn't show every extreme that they name: `routes`: within the rows of one device no expert is named more than 96 times, a bound that some block reaches; the ids of one token differ. The lengths sum to 2048; none is longer than 1536.
All inputs are finite; a program needn't handle non-finite values.
Results may differ from the reference program's by a relative error of at most 0.005.
Values may be sent and summed in bfloat16 or wider, within the bound.
A program may use at most 128 MiB of HBM per device.

```python
import math
import jax
import jax.numpy as jnp
import numpy as np
from jax import lax

D = 2048
HID = 384
TOP = 8
SEQS = 2
TOK_DEV = 128
EXPERTS = 16
TOKENS = 2048
MOST_LEN = 1536
CAP = 96
N_DP = 1
N_EXPERT = 16


def steps_of(stream_key, dims, shards, low, largest):
    def one(axis_at, shards_of):
        steps = jax.random.uniform(jax.random.fold_in(jax.random.fold_in(stream_key, 6), axis_at), (shards_of,), jnp.float32, low / len(shards), largest / len(shards))
        return jnp.repeat(jnp.exp(steps), dims[axis_at] // shards_of).reshape((-1,) + (1,) * (len(dims) - axis_at - 1))

    factor_of = one(*shards[0])
    for cut in shards[1:]:
        factor_of = factor_of * one(*cut)
    return factor_of


def length_profile(number_of, total, reach, lean):
    loads = [(1 << 20) // math.isqrt(standing ** lean) + 1 for standing in range(2, number_of + 1)]
    rest, holding = total - reach - (number_of - 1), [1] * (number_of - 1)
    while rest > 0:
        candidates = [i for i in range(number_of - 1) if holding[i] < reach]
        pool, budget = sum([loads[i] for i in candidates]), rest
        for i in candidates:
            extra = min(reach - holding[i], max(1, budget * loads[i] // pool), rest)
            holding[i] = holding[i] + extra
            rest = rest - extra
    return np.array([reach] + holding)


def ragged_sizes(stream_key, number_of, total, bound, skew):
    if number_of == 2:
        one = jax.random.randint(stream_key, (), max(1, total - bound), min(bound, total - 1) + 1)
        return jnp.stack([one, total - one])
    sizes = jnp.asarray(length_profile(number_of, total, bound, skew), jnp.int32)
    pairs = (number_of - 1) // 2
    giver, receiver = sizes[1:1 + 2 * pairs:2], sizes[2:2 + 2 * pairs:2]
    room = jnp.minimum(giver - 1, bound - receiver)
    passed = jax.random.randint(jax.random.fold_in(stream_key, 1), (pairs,), 0, 1 << 20) % (room + 1)
    sizes = sizes.at[1:1 + 2 * pairs:2].set(giver - passed).at[2:2 + 2 * pairs:2].set(receiver + passed)
    return sizes[jax.random.permutation(jax.random.fold_in(stream_key, 2), number_of)]


def deal_out(stream_key, own, number, rows, number_of, top, most, slope):
    sequence = jax.random.permutation(stream_key, number_of)
    packed, ordinary = load_shares(number_of, rows * top, most, slope, True), load_shares(number_of, rows * top, most, slope, False)
    places = jnp.arange(number_of)

    def named(sizes, rotation):
        used = int((sizes > 0).sum())
        fixed = max(1, used // 4)
        passed = fixed + (places - fixed + rotation * (used - fixed)) % max(1, number_of - fixed)
        return jnp.zeros((number_of,), jnp.int32).at[sequence[jnp.where(places < fixed, places, passed)]].set(jnp.asarray(sizes, jnp.int32))

    sizes = jnp.where(number % 4 == 0, named(packed, number // 4), named(ordinary, number - number // 4 - 1))
    mixed = jax.random.permutation(jax.random.fold_in(own, 3), number_of)
    giver, taker = mixed[0:number_of // 2 * 2:2], mixed[1:number_of // 2 * 2:2]
    slack = jnp.minimum(sizes[giver] - 1, most - sizes[taker]) // 2
    slack = jnp.where((giver == sequence[0]) | (taker == sequence[0]) | (sizes[taker] == 0), 0, jnp.maximum(slack, 0))
    passed = jax.random.randint(jax.random.fold_in(own, 4), (number_of // 2,), 0, 1 << 20) % (slack + 1)
    sizes = sizes.at[giver].add(-passed).at[taker].add(passed)
    labels = jnp.searchsorted(jnp.cumsum(sizes), jnp.arange(rows * top), side="right").astype(jnp.int32)
    listing = labels.reshape(top, rows).T
    listing = listing[jax.random.permutation(jax.random.fold_in(own, 1), rows)]
    rotation = jax.random.randint(jax.random.fold_in(own, 2), (rows, 1), 0, top)
    return jnp.take_along_axis(listing, (jnp.arange(top)[None, :] + rotation) % top, axis=1)


def load_shares(amount, total, limit, lean, full):
    portions = [(1 << 20) // math.isqrt(standing ** lean) + 1 for standing in range(1, amount + 1)]
    largest = limit if full else min(limit, max(-(-total // amount), total * portions[0] // sum(portions)))
    least = 1 if total - largest >= amount - 1 else 0
    given, spare = [largest] + [least] * (amount - 1), total - largest - least * (amount - 1)
    while spare > 0:
        candidates = [i for i in range(1, amount) if given[i] < largest] or [i for i in range(1, amount) if given[i] < limit]
        mass, budget = sum([portions[i] for i in candidates]), spare
        for i in candidates:
            more = min(limit - given[i], max(1, budget * portions[i] // mass), spare)
            given[i] = given[i] + more
            spare = spare - more
    return np.array(given)


def scatter_about(stream_key, dims, spread, limit, split=(), kind=jnp.bfloat16):
    result = jax.random.normal(stream_key, dims, jnp.float32) * spread
    if len(split) > 0:
        result = steps_of(stream_key, dims, split, -0.22, 0.18) * result
    return jnp.clip(result, min=-limit, max=limit).astype(kind)


def setup_inputs(seed: int = 0, part: int = 0) -> dict:
    key_list = jax.random.split(jax.random.key(seed), 8)
    own_keys = jax.random.split(jax.random.fold_in(key_list[7], part), 8)
    inner = scatter_about(own_keys[0], (TOKENS, TOP, HID), 0.1, 0.59765625, ((0, 16),))
    upstream = scatter_about(own_keys[1], (TOKENS, D), 1.0, 6.0, ((0, 16),))
    routes_keys = jax.random.split(jax.random.fold_in(own_keys[2], 1), TOKENS // TOK_DEV)
    routes_turns = jax.random.permutation(jax.random.fold_in(own_keys[2], 3), TOKENS // TOK_DEV)
    routes = jax.vmap(lambda own, number: deal_out(jax.random.fold_in(own_keys[2], 2), own, number, TOK_DEV, EXPERTS, TOP, CAP, 2))(routes_keys, routes_turns).reshape((TOKENS, TOP))
    gates = jnp.clip(0.2 + 0.8 * jax.random.uniform(own_keys[3], (TOKENS, TOP), jnp.float32) ** steps_of(own_keys[3], (TOKENS, TOP), ((0, 16),), -0.2, 0.2), 0.2, 1.0)
    lengths = ragged_sizes(own_keys[4], SEQS, TOKENS, MOST_LEN, 2).astype(jnp.int32)
    advantages = scatter_about(own_keys[5], (SEQS,), 1.0, 4.0, (), jnp.float32)
    down_weight = scatter_about(key_list[6], (EXPERTS, D, HID), D ** -0.5, 0.125, ((0, 16),))
    return dict(inner=inner, upstream=upstream, routes=routes, gates=gates, lengths=lengths, advantages=advantages, down_weight=down_weight)


def reference(inner, upstream, routes, gates, lengths, advantages, down_weight):
    ends = jnp.cumsum(lengths)
    position = jnp.arange(TOKENS, dtype=jnp.int32)
    seq_index = jnp.sum((position[:, None] >= ends[None, :]).astype(jnp.int32), axis=1)
    token_adv = advantages[seq_index]
    factor = (gates * token_adv[:, None]).reshape(-1)
    flat_route = routes.reshape(-1)
    order = jnp.argsort(flat_route, stable=True).astype(jnp.int32)
    counts = jax.ops.segment_sum(jnp.ones_like(flat_route), flat_route, EXPERTS).astype(jnp.int32)
    offsets = (jnp.cumsum(counts) - counts).astype(jnp.int32)
    most_rows = N_DP * N_EXPERT * CAP
    padded = jnp.concatenate([order, jnp.zeros((most_rows,), jnp.int32)])
    flat_inner = inner.reshape(-1, HID)

    def per_expert(carry, expert_id):
        index = lax.dynamic_slice(padded, (offsets[expert_id],), (most_rows,))
        live = jnp.arange(most_rows, dtype=jnp.int32) < counts[expert_id]
        token_id = index // TOP
        rows_w = (factor[index][:, None] * upstream[token_id].astype(jnp.float32)).astype(jnp.bfloat16)
        rows_w = jnp.where(live[:, None], rows_w, jnp.zeros_like(rows_w))
        rows_h = flat_inner[index]
        weight_e = down_weight[expert_id]
        grad_e = jnp.dot(rows_w.T, rows_h, preferred_element_type=jnp.float32).astype(jnp.bfloat16)
        slot_grad = jnp.dot(rows_w, weight_e, preferred_element_type=jnp.float32).astype(jnp.bfloat16)
        target = jnp.where(live, index, TOKENS * TOP)
        carry = carry.at[target].set(slot_grad)
        return carry, grad_e

    start = jnp.zeros((TOKENS * TOP + 1, HID), jnp.bfloat16)
    slots, grad_down = lax.scan(per_expert, start, jnp.arange(EXPERTS, dtype=jnp.int32))
    grad_inner = slots[:-1].reshape(TOKENS, TOP, HID)
    return grad_inner, grad_down
```

```python
import functools

import jax
import jax.numpy as jnp
from jax import lax
from jax.experimental import pallas as pl
from jax.experimental.pallas import tpu as pltpu
from jax.sharding import PartitionSpec as P


def slot_layout(routes, experts_all, capacity):
    flat_route = routes.reshape(-1)
    chosen = (flat_route[:, None] == jnp.arange(experts_all, dtype=jnp.int32)[None, :]).astype(
        jnp.int32
    )
    before = jnp.cumsum(chosen, axis=0) - chosen
    rank_in = jnp.sum(before * chosen, axis=1)
    return flat_route * capacity + rank_in


def shards(inner, upstream, routes, gates, lengths, advantages, down_weight):
    tok_rows, top_count = routes.shape
    width = upstream.shape[1]
    hidden = inner.shape[2]
    expert_devs = lax.axis_size("expert")
    local_experts = down_weight.shape[0]
    experts_all = local_experts * expert_devs
    capacity = min(tok_rows, max(2, 3 * tok_rows * top_count // (2 * experts_all)))
    first_row = (lax.axis_index("dp") * expert_devs + lax.axis_index("expert")) * tok_rows
    position = first_row + jnp.arange(tok_rows, dtype=jnp.int32)
    ends = jnp.cumsum(lengths)
    seq_index = jnp.sum((position[:, None] >= ends[None, :]).astype(jnp.int32), axis=1)
    member = seq_index[:, None] == jnp.arange(lengths.shape[0], dtype=jnp.int32)[None, :]
    token_adv = jnp.sum(jnp.where(member, advantages[None, :], 0.0), axis=1)
    factor = gates * token_adv[:, None]
    weighted = (factor[:, :, None] * upstream[:, None, :].astype(jnp.float32)).astype(jnp.bfloat16)
    target = slot_layout(routes, experts_all, capacity)
    buffer_rows = experts_all * capacity
    block_rows = local_experts * capacity
    flat_weighted = weighted.reshape(-1, width)
    flat_inner = inner.reshape(-1, hidden)
    send_h = jnp.zeros((buffer_rows, hidden), jnp.bfloat16).at[target].set(flat_inner)
    send_w = jnp.zeros((buffer_rows, width), jnp.bfloat16).at[target].set(flat_weighted)
    recv_w, recv_h = (
        lax.all_to_all(
            send_w.reshape(expert_devs, block_rows, width),
            "expert",
            split_axis=0,
            concat_axis=0,
            tiled=True,
        ),
        lax.all_to_all(
            send_h.reshape(expert_devs, block_rows, hidden),
            "expert",
            split_axis=0,
            concat_axis=0,
            tiled=True,
        ),
    )
    recv_w = recv_w.reshape(expert_devs, local_experts, capacity, width)
    recv_h = recv_h.reshape(expert_devs, local_experts, capacity, hidden)
    columns = recv_w
    back_grad = jnp.einsum(
        "sect,eth->sech",
        columns,
        lax.all_gather(down_weight, "dp", axis=1, tiled=True),
        preferred_element_type=jnp.float32,
    )
    returned = lax.all_to_all(
        back_grad.astype(jnp.bfloat16).reshape(expert_devs, block_rows, hidden),
        "expert",
        split_axis=0,
        concat_axis=0,
        tiled=True,
    )
    grad_slots = returned.reshape(buffer_rows, hidden)
    columns = recv_w
    shares = lax.psum_scatter(
        jnp.einsum("secd,sech->deh", columns, recv_h, preferred_element_type=jnp.float32),
        "dp",
        scatter_dimension=0,
        tiled=True,
    )
    grad_down = jnp.transpose(shares, (1, 0, 2)).astype(jnp.bfloat16)
    grad_inner = grad_slots[target].reshape(tok_rows, top_count, hidden)
    return (grad_inner, grad_down)


MESH = pl.DeviceIdType.MESH
CHUNKS = 2


def kernel(
    devs,
    cap,
    seqs,
    routes_t,
    gates_t,
    routes_row,
    lengths,
    advantages,
    inner,
    upstream,
    down,
    grad_inner,
    grad_down,
    up_all,
    meta_out,
    meta_in,
    inner_out,
    inner_in,
    ret_out,
    ret_in,
    weighted,
    total,
    target_row,
    target_col,
    own_sem,
    up_send,
    up_recv,
    meta_send,
    meta_recv,
    inner_send,
    inner_recv,
    ret_send,
    ret_recv,
):
    top, tok = routes_t.shape
    slots = top * tok
    hidden = down.shape[1]
    depth = devs // 4
    chips = devs // 2
    me = lax.axis_index("expert")
    core = lax.rem(me, 2)
    chip = lax.div(me, 2)
    col = lax.rem(chip, 2)
    z = lax.div(chip, 2)
    rows = tok // CHUNKS
    f32, bf16, i32 = jnp.float32, jnp.bfloat16, jnp.int32

    def iota(shape, axis):
        return lax.broadcasted_iota(i32, shape, axis)

    def device(zs, xs, cs):
        return (zs * 2 + xs) * 2 + cs

    own = pltpu.make_async_copy(upstream, up_all.at[me], own_sem)
    own.start()
    barrier = pltpu.get_barrier_semaphore()

    @pl.loop(1, devs)
    def _(i):
        peer = lax.rem(me + i, devs)
        pl.semaphore_signal(barrier, inc=1, device_id={"expert": peer}, device_id_type=MESH)

    routed = routes_t[...]
    position = me * tok + iota((1, tok), 1)
    token_adv = jnp.zeros((1, tok), f32)
    first = jnp.int32(0)
    for s in range(seqs):
        last = first + lengths[s]
        held = (position >= first) & (position < last)
        token_adv = jnp.where(held, advantages[s], token_adv)
        first = last
    factor = gates_t[...] * token_adv
    named, factors = [], []
    for e in range(devs):
        hit = routed == e
        named.append(jnp.sum(jnp.where(hit, 1.0, 0.0), axis=0, keepdims=True))
        factors.append(jnp.sum(jnp.where(hit, factor, 0.0), axis=0, keepdims=True))
    chosen = jnp.concatenate(named, axis=0)
    earlier = jnp.where(iota((tok, tok), 0) < iota((tok, tok), 1), 1.0, 0.0).astype(bf16)
    rank = jnp.dot(chosen.astype(bf16), earlier, preferred_element_type=f32)
    listed = jnp.where(chosen > 0.5, rank, -1000.0)
    line = iota((8, tok), 0)
    for e in range(devs):
        meta_out[e] = jnp.where(
            line == 0, factors[e], jnp.where(line == 1, listed[e : e + 1], 0.0)
        )
    lane, row = iota((tok, slots), 1), iota((tok, slots), 0)
    spread = jnp.where((lane >= row * top) & (lane < (row + 1) * top), 1.0, 0.0).astype(bf16)
    by_slot = jnp.dot(rank.astype(bf16), spread, preferred_element_type=f32)
    which = iota((devs, slots), 0)
    start_of = (which * cap).astype(f32)
    aim = jnp.sum(
        jnp.where(which == routes_row[...], by_slot + start_of, 0.0), axis=0, keepdims=True
    )
    aim8 = jnp.broadcast_to(aim, (8, slots))
    target_row[...] = aim8.astype(i32)
    target_col[...] = jnp.transpose(aim8).astype(i32)

    own.wait()
    pl.semaphore_wait(barrier, devs - 1)

    def up_copy(source, part, zs, kind, peer):
        block = up_all.at[source, pl.ds(part * rows, rows)]
        return pltpu.make_async_remote_copy(
            src_ref=block,
            dst_ref=block,
            send_sem=up_send.at[zs, kind, part],
            recv_sem=up_recv.at[source, part],
            device_id={"expert": peer},
            device_id_type=MESH,
        )

    def spread_on(zs, part, op):
        source = device(zs, col, core)
        up_from = (zs <= z) & (z + 1 < depth)
        down_from = (zs >= z) & (z >= 1)

        @pl.when(up_from)
        def _():
            op(up_copy(source, part, zs, 0, device(jnp.minimum(z + 1, depth - 1), col, core)))

        @pl.when(down_from)
        def _():
            op(up_copy(source, part, zs, 1, device(jnp.maximum(z - 1, 0), col, core)))

        op(up_copy(source, part, zs, 2, device(z, 1 - col, core)))
        op(up_copy(source, part, zs, 3, device(z, col, 1 - core)))

    def across(zs, part, op):
        op(up_copy(device(zs, 1 - col, core), part, zs, 4, device(z, col, 1 - core)))

    def ordered(i):
        low = jnp.minimum(z, depth - 1 - z)
        middle = jnp.where(i == 0, 1, jnp.where(i == 1, 2, jnp.where(i == 2, 0, 3)))
        near = jnp.where(low == 0, i, middle)
        return jnp.where(z < 2, near, depth - 1 - near)

    for part in range(CHUNKS):
        spread_on(z, part, lambda copy: copy.start())

    def block_copy(out, into, send, recv, peer):
        return pltpu.make_async_remote_copy(
            src_ref=out.at[peer],
            dst_ref=into.at[me],
            send_sem=send.at[peer],
            recv_sem=recv.at[me],
            device_id={"expert": peer},
            device_id_type=MESH,
        )

    def arrival(out, into, send, recv, source):
        return pltpu.make_async_remote_copy(
            src_ref=out.at[source],
            dst_ref=into.at[source],
            send_sem=send.at[source],
            recv_sem=recv.at[source],
            device_id={"expert": source},
            device_id_type=MESH,
        )

    meta_set = (meta_out, meta_in, meta_send, meta_recv)
    inner_set = (inner_out, inner_in, inner_send, inner_recv)
    ret_set = (ret_out, ret_in, ret_send, ret_recv)

    @pl.loop(1, devs)
    def _(i):
        block_copy(*meta_set, lax.rem(me + i, devs)).start()

    meta_in[me] = meta_out[me]

    def send_pair(block_set, j):
        out, into = block_set[0], block_set[1]
        for c in range(2):
            peer = j * 2 + c

            @pl.when(peer != me)
            def _():
                block_copy(*block_set, peer).start()

            @pl.when(peer == me)
            def _():
                into[me] = out[me]

    @pl.loop(0, chips)
    def _(i):
        j = lax.rem(chip + chips // 2 + i, chips)
        take = iota((2 * cap, slots), 0) + j * (2 * cap) == target_row[0:1, :]
        packed = jnp.dot(
            jnp.where(take, 1.0, 0.0).astype(bf16), inner[...], preferred_element_type=f32
        )
        inner_out[pl.ds(j * 2, 2)] = packed.astype(bf16).reshape(2, cap, hidden)
        send_pair(inner_set, j)

    total[...] = jnp.zeros_like(total)

    def wait_pair(block_set, j):
        for c in range(2):
            source = j * 2 + c

            @pl.when(source != me)
            def _():
                arrival(*block_set, source).wait_recv()

    def wait_up(source):
        for part in range(CHUNKS):
            up_copy(source, part, 0, 0, device(z, col, 1 - core)).wait_recv()

    def compute(zs, xs):
        j = zs * 2 + xs
        wait_up(device(zs, xs, 1 - core))
        wait_pair(meta_set, j)
        pair = pl.ds(j * 2, 2)
        notes = meta_in[pair]
        columns = jnp.concatenate([jnp.transpose(notes[0]), jnp.transpose(notes[1])], axis=0)
        second = iota((2 * tok, 1), 0) >= tok
        scale = columns[:, 0:1]
        rank_col = (columns[:, 1:2] + jnp.where(second, float(cap), 0.0)).astype(i32)
        rank_row = jnp.concatenate([notes[0][1:2], notes[1][1:2] + float(cap)], axis=1).astype(i32)
        block = up_all[pair].reshape(2 * tok, up_all.shape[2])
        weighted[...] = (scale * block.astype(f32)).astype(bf16)
        slot_grad = jnp.dot(weighted[...], down[...], preferred_element_type=f32).astype(bf16)
        pick = jnp.where(iota((2 * cap, 2 * tok), 0) == rank_row, 1.0, 0.0).astype(bf16)
        packed = jnp.dot(pick, slot_grad, preferred_element_type=f32).astype(bf16)
        ret_out[pair] = packed.reshape(2, cap, hidden)
        send_pair(ret_set, j)
        wait_pair(inner_set, j)
        place = jnp.where(iota((2 * tok, 2 * cap), 1) == rank_col, 1.0, 0.0).astype(bf16)
        rows_h = jnp.dot(
            place, inner_in[pair].reshape(2 * cap, hidden), preferred_element_type=f32
        ).astype(bf16)
        total[...] += lax.dot_general(
            weighted[...], rows_h, (((0,), (0,)), ((), ())), preferred_element_type=f32
        )

    @pl.loop(0, depth + 2)
    def _(i):
        @pl.when((i >= 1) & (i < depth))
        def _():
            zs = ordered(i)
            for part in range(CHUNKS):
                up_copy(device(zs, col, core), part, 0, 0, device(z, 1 - col, core)).wait_recv()
                spread_on(zs, part, lambda copy: copy.start())

        @pl.when((i >= 1) & (i < depth + 1))
        def _():
            zs = ordered(i - 1)
            for part in range(CHUNKS):
                up_copy(device(zs, 1 - col, core), part, 0, 0, device(z, 1 - col, core)).wait_recv()
                across(zs, part, lambda copy: copy.start())

        @pl.loop(0, 2)
        def _(p):
            lag = i - 1 - p

            @pl.when((lag >= 0) & (lag < depth))
            def _():
                compute(ordered(lag), jnp.where(p == 0, col, 1 - col))

    grad_down[...] = total[...].astype(bf16)

    @pl.loop(1, devs)
    def _(i):
        arrival(*ret_set, lax.rem(me + i, devs)).wait_recv()

    tile = 256

    @pl.loop(0, slots // tile)
    def _(i):
        at = pl.ds(pl.multiple_of(i * tile, tile), tile)
        put = iota((tile, devs * cap), 1) == target_col[at, 0:1]
        grad_inner[at, :] = jnp.dot(
            jnp.where(put, 1.0, 0.0).astype(bf16),
            ret_in[...].reshape(devs * cap, hidden),
            preferred_element_type=f32,
        ).astype(bf16)

    @pl.loop(1, devs)
    def _(i):
        peer = lax.rem(me + i, devs)
        block_copy(*meta_set, peer).wait_send()
        block_copy(*inner_set, peer).wait_send()
        block_copy(*ret_set, peer).wait_send()

    @pl.loop(0, depth)
    def _(zs):
        for part in range(CHUNKS):
            spread_on(zs, part, lambda copy: copy.wait_send())
            across(zs, part, lambda copy: copy.wait_send())


def fused(inner, upstream, routes, gates, lengths, advantages, down_weight):
    tok, top = routes.shape
    width = upstream.shape[1]
    hidden = inner.shape[2]
    devs = lax.axis_size("expert")
    slots = tok * top
    cap = min(tok, max(2, 3 * slots // (2 * devs)))
    bf16, f32, i32 = jnp.bfloat16, jnp.float32, jnp.int32
    vmem = pl.BlockSpec(memory_space=pltpu.VMEM)
    smem = pl.BlockSpec(memory_space=pltpu.SMEM)
    dma = pltpu.SemaphoreType.DMA
    flops = 4 * devs * tok * width * hidden
    grad_inner, grad_down = pl.pallas_call(
        functools.partial(kernel, devs, cap, lengths.shape[0]),
        out_shape=(
            jax.ShapeDtypeStruct((slots, hidden), bf16),
            jax.ShapeDtypeStruct((width, hidden), bf16),
        ),
        in_specs=[vmem, vmem, vmem, smem, smem, vmem, pl.BlockSpec(memory_space=pl.ANY), vmem],
        out_specs=(vmem, vmem),
        scratch_shapes=[
            pltpu.VMEM((devs, tok, width), bf16),
            pltpu.VMEM((devs, 8, tok), f32),
            pltpu.VMEM((devs, 8, tok), f32),
            pltpu.VMEM((devs, cap, hidden), bf16),
            pltpu.VMEM((devs, cap, hidden), bf16),
            pltpu.VMEM((devs, cap, hidden), bf16),
            pltpu.VMEM((devs, cap, hidden), bf16),
            pltpu.VMEM((2 * tok, width), bf16),
            pltpu.VMEM((width, hidden), f32),
            pltpu.VMEM((8, slots), i32),
            pltpu.VMEM((slots, 8), i32),
            dma,
            dma((devs // 4, 5, CHUNKS)),
            dma((devs, CHUNKS)),
            dma((devs,)),
            dma((devs,)),
            dma((devs,)),
            dma((devs,)),
            dma((devs,)),
            dma((devs,)),
        ],
        compiler_params=pltpu.CompilerParams(
            collective_id=0, has_side_effects=True, vmem_limit_bytes=48 * 1024 * 1024
        ),
        cost_estimate=pl.CostEstimate(flops=flops, bytes_accessed=8_000_000, transcendentals=0),
    )(
        routes.T,
        gates.T,
        routes.reshape(1, slots),
        lengths,
        advantages,
        inner.reshape(slots, hidden),
        upstream,
        down_weight.reshape(width, hidden),
    )
    return grad_inner.reshape(tok, top, hidden), grad_down.reshape(1, width, hidden)


def solution(mesh):
    gathered = mesh.shape["dp"] == 1 and mesh.shape["expert"] == 16
    body = fused if gathered else shards
    return jax.shard_map(
        body,
        mesh=mesh,
        in_specs=(
            P(("groups", "dp", "expert"), None, None),
            P(("groups", "dp", "expert"), None),
            P(("groups", "dp", "expert"), None),
            P(("groups", "dp", "expert"), None),
            P("groups"),
            P("groups"),
            P("expert", "dp", None),
        ),
        out_specs=(P(("groups", "dp", "expert"), None, None), P(("groups", "expert"), "dp", None)),
        check_vma=False,
    )
```

```python
import functools

import jax
import jax.numpy as jnp
from jax import lax
from jax.experimental import pallas as pl
from jax.experimental.pallas import tpu as pltpu
from jax.sharding import PartitionSpec as P


def slot_layout(routes, experts_all, capacity):
    flat_route = routes.reshape(-1)
    chosen = (flat_route[:, None] == jnp.arange(experts_all, dtype=jnp.int32)[None, :]).astype(
        jnp.int32
    )
    before = jnp.cumsum(chosen, axis=0) - chosen
    rank_in = jnp.sum(before * chosen, axis=1)
    return flat_route * capacity + rank_in


def shards(inner, upstream, routes, gates, lengths, advantages, down_weight):
    tok_rows, top_count = routes.shape
    width = upstream.shape[1]
    hidden = inner.shape[2]
    expert_devs = lax.axis_size("expert")
    local_experts = down_weight.shape[0]
    experts_all = local_experts * expert_devs
    capacity = min(tok_rows, max(2, 3 * tok_rows * top_count // (2 * experts_all)))
    first_row = (lax.axis_index("dp") * expert_devs + lax.axis_index("expert")) * tok_rows
    position = first_row + jnp.arange(tok_rows, dtype=jnp.int32)
    ends = jnp.cumsum(lengths)
    seq_index = jnp.sum((position[:, None] >= ends[None, :]).astype(jnp.int32), axis=1)
    member = seq_index[:, None] == jnp.arange(lengths.shape[0], dtype=jnp.int32)[None, :]
    token_adv = jnp.sum(jnp.where(member, advantages[None, :], 0.0), axis=1)
    factor = gates * token_adv[:, None]
    weighted = (factor[:, :, None] * upstream[:, None, :].astype(jnp.float32)).astype(jnp.bfloat16)
    target = slot_layout(routes, experts_all, capacity)
    buffer_rows = experts_all * capacity
    block_rows = local_experts * capacity
    flat_weighted = weighted.reshape(-1, width)
    flat_inner = inner.reshape(-1, hidden)
    send_h = jnp.zeros((buffer_rows, hidden), jnp.bfloat16).at[target].set(flat_inner)
    send_w = jnp.zeros((buffer_rows, width), jnp.bfloat16).at[target].set(flat_weighted)
    recv_w, recv_h = (
        lax.all_to_all(
            send_w.reshape(expert_devs, block_rows, width),
            "expert",
            split_axis=0,
            concat_axis=0,
            tiled=True,
        ),
        lax.all_to_all(
            send_h.reshape(expert_devs, block_rows, hidden),
            "expert",
            split_axis=0,
            concat_axis=0,
            tiled=True,
        ),
    )
    recv_w = recv_w.reshape(expert_devs, local_experts, capacity, width)
    recv_h = recv_h.reshape(expert_devs, local_experts, capacity, hidden)
    columns = recv_w
    back_grad = jnp.einsum(
        "sect,eth->sech",
        columns,
        lax.all_gather(down_weight, "dp", axis=1, tiled=True),
        preferred_element_type=jnp.float32,
    )
    returned = lax.all_to_all(
        back_grad.astype(jnp.bfloat16).reshape(expert_devs, block_rows, hidden),
        "expert",
        split_axis=0,
        concat_axis=0,
        tiled=True,
    )
    grad_slots = returned.reshape(buffer_rows, hidden)
    columns = recv_w
    shares = lax.psum_scatter(
        jnp.einsum("secd,sech->deh", columns, recv_h, preferred_element_type=jnp.float32),
        "dp",
        scatter_dimension=0,
        tiled=True,
    )
    grad_down = jnp.transpose(shares, (1, 0, 2)).astype(jnp.bfloat16)
    grad_inner = grad_slots[target].reshape(tok_rows, top_count, hidden)
    return (grad_inner, grad_down)


MESH = pl.DeviceIdType.MESH
CHUNKS = 4
LATE = 3
VMEM_BYTES = 64 * 1024 * 1024 - 64 * 1024


def kernel(
    devs,
    cap,
    seqs,
    routes_hbm,
    gates_hbm,
    lengths_hbm,
    advantages_hbm,
    inner_hbm,
    upstream,
    down_hbm,
    grad_inner_hbm,
    grad_down_hbm,
    grad_inner,
    grad_down,
    up_all,
    meta_out,
    meta_in,
    inner_out,
    inner_in,
    ret_out,
    ret_in,
    weighted,
    total,
    target_row,
    target_col,
    routes,
    gates,
    lengths,
    advantages,
    inner,
    down,
    own_sem,
    stage_sem,
    out_sem,
    up_send,
    up_recv,
    meta_send,
    meta_recv,
    inner_send,
    inner_recv,
    ret_send,
    ret_recv,
):
    top, tok = routes.shape
    slots = top * tok
    hidden = down.shape[1]
    depth = devs // 4
    chips = devs // 2
    me = lax.axis_index("expert")
    core = lax.rem(me, 2)
    chip = lax.div(me, 2)
    col = lax.rem(chip, 2)
    z = lax.div(chip, 2)
    rows = tok // CHUNKS
    f32, bf16, i32 = jnp.float32, jnp.bfloat16, jnp.int32

    def iota(shape, axis):
        return lax.broadcasted_iota(i32, shape, axis)

    def device(zs, xs, cs):
        return (zs * 2 + xs) * 2 + cs

    own = pltpu.make_async_copy(upstream, up_all.at[me], own_sem)
    own.start()
    staged = [
        pltpu.make_async_copy(far, near, stage_sem.at[i])
        for i, (far, near) in enumerate(
            (
                (routes_hbm, routes),
                (gates_hbm, gates),
                (lengths_hbm, lengths),
                (advantages_hbm, advantages),
                (inner_hbm, inner),
                (down_hbm, down),
            )
        )
    ]
    for copy in staged:
        copy.start()
    barrier = pltpu.get_barrier_semaphore()

    @pl.loop(1, devs)
    def _(i):
        peer = lax.rem(me + i, devs)
        pl.semaphore_signal(barrier, inc=1, device_id={"expert": peer}, device_id_type=MESH)

    own.wait()
    pl.semaphore_wait(barrier, devs - 1)

    def up_copy(source, part, zs, kind, peer):
        block = up_all.at[source, pl.ds(part * rows, rows)]
        return pltpu.make_async_remote_copy(
            src_ref=block,
            dst_ref=block,
            send_sem=up_send.at[zs, kind, part],
            recv_sem=up_recv.at[source, part],
            device_id={"expert": peer},
            device_id_type=MESH,
        )

    def spread_on(zs, part, op):
        source = device(zs, col, core)
        up_from = (zs <= z) & (z + 1 < depth)
        down_from = (zs >= z) & (z >= 1)

        @pl.when(up_from)
        def _():
            op(up_copy(source, part, zs, 0, device(jnp.minimum(z + 1, depth - 1), col, core)))

        @pl.when(down_from)
        def _():
            op(up_copy(source, part, zs, 1, device(jnp.maximum(z - 1, 0), col, core)))

        op(up_copy(source, part, zs, 2, device(z, 1 - col, core)))
        op(up_copy(source, part, zs, 3, device(z, col, 1 - core)))

    def across(zs, part, op):
        op(up_copy(device(zs, 1 - col, core), part, zs, 4, device(z, col, 1 - core)))

    def ordered(i):
        low = jnp.minimum(z, depth - 1 - z)
        middle = jnp.where(i == 0, 1, jnp.where(i == 1, 2, jnp.where(i == 2, 0, 3)))
        near = jnp.where(low == 0, i, middle)
        return jnp.where(z < 2, near, depth - 1 - near)

    for part in range(CHUNKS):
        spread_on(z, part, lambda copy: copy.start())

    for copy in staged[:4]:
        copy.wait()
    routed = routes[...]
    position = me * tok + iota((1, tok), 1)
    token_adv = jnp.zeros((1, tok), f32)
    first = jnp.int32(0)
    for s in range(seqs):
        last = first + lengths[s]
        held = (position >= first) & (position < last)
        token_adv = jnp.where(held, advantages[s], token_adv)
        first = last
    factor = gates[...] * token_adv
    named, factors = [], []
    for e in range(devs):
        hit = routed == e
        named.append(jnp.sum(jnp.where(hit, 1.0, 0.0), axis=0, keepdims=True))
        factors.append(jnp.sum(jnp.where(hit, factor, 0.0), axis=0, keepdims=True))
    chosen = jnp.concatenate(named, axis=0)
    earlier = jnp.where(iota((tok, tok), 0) < iota((tok, tok), 1), 1.0, 0.0).astype(bf16)
    rank = jnp.dot(chosen.astype(bf16), earlier, preferred_element_type=f32)
    listed = jnp.where(chosen > 0.5, rank, -1000.0)
    line = iota((8, tok), 0)
    for e in range(devs):
        meta_out[e] = jnp.where(
            line == 0, factors[e], jnp.where(line == 1, listed[e : e + 1], 0.0)
        )
    lane, row = iota((tok, slots), 1), iota((tok, slots), 0)
    spread = jnp.where((lane >= row * top) & (lane < (row + 1) * top), 1.0, 0.0).astype(bf16)
    by_slot = jnp.dot(rank.astype(bf16), spread, preferred_element_type=f32)
    place_in = iota((top, slots), 1) & (top - 1)
    repeated = jnp.dot(routed.astype(f32).astype(bf16), spread, preferred_element_type=f32)
    routes_row = jnp.sum(
        jnp.where(place_in == iota((top, slots), 0), repeated, 0.0), axis=0, keepdims=True
    ).astype(i32)
    which = iota((devs, slots), 0)
    start_of = (which * cap).astype(f32)
    aim = jnp.sum(
        jnp.where(which == routes_row, by_slot + start_of, 0.0), axis=0, keepdims=True
    )
    aim8 = jnp.broadcast_to(aim, (8, slots))
    target_row[...] = aim8.astype(i32)
    target_col[...] = jnp.transpose(aim8).astype(i32)

    def block_copy(out, into, send, recv, peer):
        return pltpu.make_async_remote_copy(
            src_ref=out.at[peer],
            dst_ref=into.at[me],
            send_sem=send.at[peer],
            recv_sem=recv.at[me],
            device_id={"expert": peer},
            device_id_type=MESH,
        )

    def arrival(out, into, send, recv, source):
        return pltpu.make_async_remote_copy(
            src_ref=out.at[source],
            dst_ref=into.at[source],
            send_sem=send.at[source],
            recv_sem=recv.at[source],
            device_id={"expert": source},
            device_id_type=MESH,
        )

    meta_set = (meta_out, meta_in, meta_send, meta_recv)
    inner_set = (inner_out, inner_in, inner_send, inner_recv)
    ret_set = (ret_out, ret_in, ret_send, ret_recv)

    @pl.loop(1, devs)
    def _(i):
        block_copy(*meta_set, lax.rem(me + i, devs)).start()

    meta_in[me] = meta_out[me]

    def send_pair(block_set, j):
        out, into = block_set[0], block_set[1]
        for c in range(2):
            peer = j * 2 + c

            @pl.when(peer != me)
            def _():
                block_copy(*block_set, peer).start()

            @pl.when(peer == me)
            def _():
                into[me] = out[me]

    staged[4].wait()

    @pl.loop(0, chips)
    def _(i):
        zs = lax.rem(z + i + 1, depth)
        xs = jnp.where(i < depth, col, 1 - col)
        j = zs * 2 + xs
        take = iota((2 * cap, slots), 0) + j * (2 * cap) == target_row[0:1, :]
        packed = jnp.dot(
            jnp.where(take, 1.0, 0.0).astype(bf16), inner[...], preferred_element_type=f32
        )
        inner_out[pl.ds(j * 2, 2)] = packed.astype(bf16).reshape(2, cap, hidden)

        @pl.when(xs == col)
        def _():
            send_pair(inner_set, j)

    total[...] = jnp.zeros_like(total)
    staged[5].wait()

    def wait_pair(block_set, j):
        for c in range(2):
            source = j * 2 + c

            @pl.when(source != me)
            def _():
                arrival(*block_set, source).wait_recv()

    def wait_up(source):
        for part in range(CHUNKS):
            up_copy(source, part, 0, 0, device(z, col, 1 - core)).wait_recv()

    def compute(zs, xs):
        j = zs * 2 + xs
        wait_up(device(zs, xs, 1 - core))
        wait_pair(meta_set, j)
        pair = pl.ds(j * 2, 2)
        notes = meta_in[pair]
        columns = jnp.concatenate([jnp.transpose(notes[0]), jnp.transpose(notes[1])], axis=0)
        scale = columns[:, 0:1]
        rank_row = jnp.concatenate([notes[0][1:2], notes[1][1:2] + float(cap)], axis=1).astype(i32)
        block = up_all[pair].reshape(2 * tok, up_all.shape[2])
        weighted[j] = (scale * block.astype(f32)).astype(bf16)
        slot_grad = jnp.dot(weighted[j], down[...], preferred_element_type=f32).astype(bf16)
        pick = jnp.where(iota((2 * cap, 2 * tok), 0) == rank_row, 1.0, 0.0).astype(bf16)
        packed = jnp.dot(pick, slot_grad, preferred_element_type=f32).astype(bf16)
        ret_out[pair] = packed.reshape(2, cap, hidden)
        send_pair(ret_set, j)

    def add_up(j):
        wait_pair(inner_set, j)
        pair = pl.ds(j * 2, 2)
        notes = meta_in[pair]
        ranks = jnp.concatenate([jnp.transpose(notes[0]), jnp.transpose(notes[1])], axis=0)
        second = iota((2 * tok, 1), 0) >= tok
        rank_col = (ranks[:, 1:2] + jnp.where(second, float(cap), 0.0)).astype(i32)
        place = jnp.where(iota((2 * tok, 2 * cap), 1) == rank_col, 1.0, 0.0).astype(bf16)
        rows_h = jnp.dot(
            place, inner_in[pair].reshape(2 * cap, hidden), preferred_element_type=f32
        ).astype(bf16)
        total[...] += lax.dot_general(
            weighted[j], rows_h, (((0,), (0,)), ((), ())), preferred_element_type=f32
        )

    outer = (z == 0) | (z == depth - 1)

    @pl.loop(1, depth + 2)
    def _(i):
        @pl.loop(0, 2)
        def _(q):
            number = jnp.where(outer, i, i + jnp.where(i == 1, q, 1))

            @pl.when((number < depth) & ((q == 0) | ((i == 1) & jnp.logical_not(outer))))
            def _():
                zs = ordered(number)
                for part in range(CHUNKS):
                    up_copy(device(zs, col, core), part, 0, 0, device(z, 1 - col, core)).wait_recv()
                    spread_on(zs, part, lambda copy: copy.start())

        @pl.when(i == LATE)
        def _():
            @pl.loop(0, depth)
            def _(step):
                send_pair(inner_set, lax.rem(z + step + 1, depth) * 2 + 1 - col)

        @pl.when(i < depth + 1)
        def _():
            zs = ordered(i - 1)
            for part in range(CHUNKS):
                up_copy(device(zs, 1 - col, core), part, 0, 0, device(z, 1 - col, core)).wait_recv()
                across(zs, part, lambda copy: copy.start())

        @pl.loop(0, 2)
        def _(p):
            lag = i - 1 - p

            @pl.when((lag >= 0) & (lag < depth))
            def _():
                compute(ordered(lag), jnp.where(p == 0, col, 1 - col))

    @pl.loop(0, chips)
    def _(i):
        add_up(ordered(lax.rem(i, depth)) * 2 + jnp.where(i < depth, col, 1 - col))

    grad_down[...] = total[...].astype(bf16)
    down_out = pltpu.make_async_copy(grad_down, grad_down_hbm, out_sem.at[0])
    down_out.start()

    @pl.loop(1, devs)
    def _(i):
        arrival(*ret_set, lax.rem(me + i, devs)).wait_recv()

    tile = 256

    def tile_out(i):
        at = pl.ds(pl.multiple_of(i * tile, tile), tile)
        return pltpu.make_async_copy(grad_inner.at[at], grad_inner_hbm.at[at], out_sem.at[1 + i])

    @pl.loop(0, slots // tile)
    def _(i):
        at = pl.ds(pl.multiple_of(i * tile, tile), tile)
        put = iota((tile, devs * cap), 1) == target_col[at, 0:1]
        grad_inner[at, :] = jnp.dot(
            jnp.where(put, 1.0, 0.0).astype(bf16),
            ret_in[...].reshape(devs * cap, hidden),
            preferred_element_type=f32,
        ).astype(bf16)
        tile_out(i).start()

    @pl.loop(1, devs)
    def _(i):
        peer = lax.rem(me + i, devs)
        block_copy(*meta_set, peer).wait_send()
        block_copy(*inner_set, peer).wait_send()
        block_copy(*ret_set, peer).wait_send()

    @pl.loop(0, depth)
    def _(zs):
        for part in range(CHUNKS):
            spread_on(zs, part, lambda copy: copy.wait_send())
            across(zs, part, lambda copy: copy.wait_send())

    down_out.wait()

    @pl.loop(0, slots // tile)
    def _(i):
        tile_out(i).wait()


def fused(inner, upstream, routes, gates, lengths, advantages, down_weight):
    tok, top = routes.shape
    width = upstream.shape[1]
    hidden = inner.shape[2]
    devs = lax.axis_size("expert")
    slots = tok * top
    cap = min(tok, max(2, 3 * slots // (2 * devs)))
    bf16, f32, i32 = jnp.bfloat16, jnp.float32, jnp.int32
    hbm = pl.BlockSpec(memory_space=pltpu.HBM)
    dma = pltpu.SemaphoreType.DMA
    flops = 4 * devs * tok * width * hidden
    grad_inner, grad_down = pl.pallas_call(
        functools.partial(kernel, devs, cap, lengths.shape[0]),
        out_shape=(
            jax.ShapeDtypeStruct((slots, hidden), bf16),
            jax.ShapeDtypeStruct((width, hidden), bf16),
        ),
        in_specs=[hbm] * 7,
        out_specs=(hbm, hbm),
        scratch_shapes=[
            pltpu.VMEM((slots, hidden), bf16),
            pltpu.VMEM((width, hidden), bf16),
            pltpu.VMEM((devs, tok, width), bf16),
            pltpu.VMEM((devs, 8, tok), f32),
            pltpu.VMEM((devs, 8, tok), f32),
            pltpu.VMEM((devs, cap, hidden), bf16),
            pltpu.VMEM((devs, cap, hidden), bf16),
            pltpu.VMEM((devs, cap, hidden), bf16),
            pltpu.VMEM((devs, cap, hidden), bf16),
            pltpu.VMEM((devs // 2, 2 * tok, width), bf16),
            pltpu.VMEM((width, hidden), f32),
            pltpu.VMEM((8, slots), i32),
            pltpu.VMEM((slots, 8), i32),
            pltpu.VMEM((top, tok), i32),
            pltpu.VMEM((top, tok), f32),
            pltpu.SMEM(lengths.shape, i32),
            pltpu.SMEM(advantages.shape, f32),
            pltpu.VMEM((slots, hidden), bf16),
            pltpu.VMEM((width, hidden), bf16),
            dma,
            dma((6,)),
            dma((1 + slots // 256,)),
            dma((devs // 4, 5, CHUNKS)),
            dma((devs, CHUNKS)),
            dma((devs,)),
            dma((devs,)),
            dma((devs,)),
            dma((devs,)),
            dma((devs,)),
            dma((devs,)),
        ],
        compiler_params=pltpu.CompilerParams(
            collective_id=0, has_side_effects=True, vmem_limit_bytes=VMEM_BYTES
        ),
        cost_estimate=pl.CostEstimate(flops=flops, bytes_accessed=8_000_000, transcendentals=0),
    )(
        routes.T,
        gates.T,
        lengths,
        advantages,
        inner.reshape(slots, hidden),
        upstream,
        down_weight.reshape(width, hidden),
    )
    return grad_inner.reshape(tok, top, hidden), grad_down.reshape(1, width, hidden)

def solution(mesh):
    gathered = mesh.shape["dp"] == 1 and mesh.shape["expert"] == 16
    body = fused if gathered else shards
    return jax.shard_map(
        body,
        mesh=mesh,
        in_specs=(
            P(("groups", "dp", "expert"), None, None),
            P(("groups", "dp", "expert"), None),
            P(("groups", "dp", "expert"), None),
            P(("groups", "dp", "expert"), None),
            P("groups"),
            P("groups"),
            P("expert", "dp", None),
        ),
        out_specs=(P(("groups", "dp", "expert"), None, None), P(("groups", "expert"), "dp", None)),
        check_vma=False,
    )
```
